32 devices in a mesh: section: 2 (over core), dp: 16 (over z, y, x).
Axes of the slice: x: 2, y: 2, z: 4, core: 2. Of those that a mesh axis runs over, the one named last changes fastest.
Arguments:
- tokens: bfloat16 [2, 16, 128, 768], P(None, 'dp'), may hold values from -6 to 6
- cotangent: bfloat16 [2, 16, 128, 768], P(None, 'dp'), may hold values from -6 to 6
- lengths: int32 [2, 16], P(None, 'dp'), may hold values from 16 to 128, as said below
- qkv_weight: bfloat16 [2, 768, 2304], P('section', 'dp'), may hold values from -0.21875 to 0.21875
- out_weight: bfloat16 [2, 768, 768], P('section', 'dp'), may hold values from -1.75 to 1.75
- up_weight: bfloat16 [2, 768, 3072], P('section', 'dp'), may hold values from -0.21875 to 0.21875
- down_weight: bfloat16 [2, 3072, 768], P('section', 'dp'), may hold values from -0.109375 to 0.109375
- up_bias: bfloat16 [2, 3072], P('section', 'dp'), may hold values from -1.75 to 1.75
- norm_gains: bfloat16 [2, 2, 768], P('section', None, 'dp'), may hold values from 0.25 to 1.75
- biases: bfloat16 [2, 6, 768], P('section', None, 'dp'), may hold values from -1.75 to 1.75
Outputs:
- layer_outputs: bfloat16 [2, 2, 16, 128, 768], P('section', None, 'dp')
- input_grads: float32 [2, 2, 16, 128, 768], P('section', None, 'dp')
- qkv_grad: float32 [2, 768, 2304], P('section', 'dp')
- out_grad: float32 [2, 768, 768], P('section', 'dp')
- up_grad: float32 [2, 768, 3072], P('section', 'dp')
- down_grad: float32 [2, 3072, 768], P('section', 'dp')
- up_bias_grad: float32 [2, 3072], P('section', 'dp')
- gains_grad: float32 [2, 2, 768], P('section', None, 'dp')
- biases_grad: float32 [2, 6, 768], P('section', None, 'dp')
The draws below stay inside these ranges and needn't reach their ends.
Inputs may be any that keep to these rules, and one draw needn't show every extreme that they name: `lengths`: in every draw some clip has all 128 frames valid.
All inputs are finite; a program needn't handle non-finite values.
Results may differ from the reference program's by a relative error of at most 0.017.
Values may be sent and summed in bfloat16 or wider, within the bound.
A program may use at most 320 MiB of HBM per device.

```python
import math
import jax
import jax.numpy as jnp
from jax import lax

D = 768
H = 12
HD = 64
FF = 3072
LEN = 128
MB = 2
CLIPS = 16


def draw_lengths(key, part):
    key = jax.random.fold_in(key, 11)
    first_key, second_key = jax.random.split(key)
    drawn = jax.random.randint(first_key, (MB * CLIPS,), LEN // 8, LEN + 1)
    chosen = jax.random.randint(second_key, (), 0, MB * CLIPS)
    filled = jnp.where(jnp.arange(MB * CLIPS) == chosen, LEN, drawn)
    return filled.reshape(MB, CLIPS).astype(jnp.int32)


def levels(rng, shape, cuts, smallest, top_value):
    gain, own = 1.0, jax.random.fold_in(rng, 6)
    for dim, shards_of in cuts:
        draws = jnp.exp(jax.random.uniform(jax.random.fold_in(own, dim), (shards_of,), jnp.float32, smallest / len(cuts), top_value / len(cuts)))
        gain = gain * jnp.repeat(draws, shape[dim] // shards_of).reshape([-1 if axis == dim else 1 for axis in range(len(shape))])
    return gain


def gaussian(key, shape, width, most, shards=(), kind=jnp.bfloat16):
    result = jax.random.normal(key, shape, jnp.float32) * width
    if len(shards) > 0:
        result = levels(key, shape, shards, -0.22, 0.18) * result
    return jnp.clip(result, min=-most, max=most).astype(kind)


def setup_inputs(seed: int = 0) -> dict:
    key_list = jax.random.split(jax.random.key(seed), 11)
    tokens = gaussian(key_list[0], (MB, CLIPS, LEN, D), 1.0, 6.0, ((1, 16),))
    cotangent = gaussian(key_list[1], (MB, CLIPS, LEN, D), 1.0, 6.0, ((1, 16),))
    lengths = draw_lengths(jax.random.fold_in(key_list[10], 71), 0)
    qkv_weight = gaussian(key_list[3], (2, D, 3 * D), D ** -0.5, 0.21875, ((0, 2), (1, 16)))
    out_weight = gaussian(key_list[4], (2, D, D), (max(1, 2 * D // LEN)) ** -0.5, 1.75, ((0, 2), (1, 16)))
    up_weight = gaussian(key_list[5], (2, D, FF), D ** -0.5, 0.21875, ((0, 2), (1, 16)))
    down_weight = gaussian(key_list[6], (2, FF, D), FF ** -0.5, 0.109375, ((0, 2), (1, 16)))
    up_bias = gaussian(key_list[7], (2, FF), 0.3, 1.75, ((0, 2), (1, 16)))
    norm_gains = jnp.clip(1.0 + 0.15 * jax.random.normal(key_list[8], (2, 2, D), jnp.float32), 0.25, 1.75).astype(jnp.bfloat16)
    biases = gaussian(key_list[9], (2, 6, D), 0.3, 1.75, ((0, 2), (2, 16)))
    return {"tokens": tokens, "cotangent": cotangent, "lengths": lengths, "qkv_weight": qkv_weight, "out_weight": out_weight, "up_weight": up_weight, "down_weight": down_weight, "up_bias": up_bias, "norm_gains": norm_gains, "biases": biases}


@jax.custom_vjp
def low(v):
    return lax.optimization_barrier(v.astype(jnp.bfloat16)).astype(jnp.float32)

@jax.custom_vjp
def low_back(v):
    return v

def low_keep(v):
    return (low(v), None)

def low_pass(kept, grad):
    return (grad,)

def back_keep(v):
    return (v, None)

def back_low(kept, grad):
    return (low(grad),)
low.defvjp(low_keep, low_pass)
low_back.defvjp(back_keep, back_low)
EPSILON = 1e-05
MASKED = -1e+30

def product(left, right):
    return jnp.dot(left, right, precision=lax.Precision.HIGHEST)

def layer_norm(values, scale_gain, offset):
    average = lax.optimization_barrier(jnp.mean(values, -1, keepdims=True))
    centred = values - average
    variance = lax.optimization_barrier(jnp.mean(centred * centred, -1, keepdims=True))
    return centred * lax.rsqrt(variance + EPSILON) * scale_gain + offset

def attend_block(query_block, key_heads, value_heads, visible):
    scaling = 1.0 / math.sqrt(HD)
    scores = jnp.einsum('qhd,khd->hqk', query_block, key_heads, precision=lax.Precision.HIGHEST) * scaling
    scores = low_back(scores)
    scores = jnp.where(visible[None, None, :], scores, MASKED)
    largest = lax.optimization_barrier(jnp.max(scores, -1, keepdims=True))
    exponent = jnp.exp(scores - largest)
    probability = low(exponent / lax.optimization_barrier(jnp.sum(exponent, -1, keepdims=True)))
    return jnp.einsum('hqk,khd->qhd', probability, value_heads, precision=lax.Precision.HIGHEST)

def encoder_layer(inputs, params, length):
    qkv_weight, out_weight, up_weight, down_weight, up_bias, norm_gains, biases = params
    normed = low(layer_norm(inputs, norm_gains[0], biases[0]))
    mixed = product(normed, qkv_weight)
    query = low_back(low(mixed[:, :D] + biases[1]))
    keyed = low_back(low(mixed[:, D:2 * D]))
    valued = low_back(low(mixed[:, 2 * D:] + biases[2]))
    block_rows = min(512, LEN)
    query_blocks = query.reshape(LEN // block_rows, block_rows, H, HD)
    key_heads = keyed.reshape(LEN, H, HD)
    value_heads = valued.reshape(LEN, H, HD)
    visible = jnp.arange(LEN) < length
    checked = jax.checkpoint(attend_block)
    context = lax.map(lambda block: checked(block, key_heads, value_heads, visible), query_blocks)
    context = low_back(low(context.reshape(LEN, D)))
    branch = low_back(product(context, out_weight) + biases[3])
    hidden = inputs + branch
    normed_two = low(layer_norm(hidden, norm_gains[1], biases[4]))
    upper = low_back(product(normed_two, up_weight) + up_bias)
    active = low(jax.nn.gelu(upper, approximate=False))
    branch_two = low_back(product(active, down_weight) + biases[5])
    return hidden + branch_two

def reference(tokens, cotangent, lengths, qkv_weight, out_weight, up_weight, down_weight, up_bias, norm_gains, biases):
    arrays = (qkv_weight, out_weight, up_weight, down_weight, up_bias, norm_gains, biases)
    first_params = tuple((entry[0].astype(jnp.float32) for entry in arrays))
    second_params = tuple((entry[1].astype(jnp.float32) for entry in arrays))
    flat_tokens = tokens.reshape(MB * CLIPS, LEN, D)
    flat_cot = cotangent.reshape(MB * CLIPS, LEN, D)
    flat_lengths = lengths.reshape(MB * CLIPS)
    zeros = jax.tree.map(jnp.zeros_like, (first_params, second_params))

    def one_clip(totals, record):
        inputs, grad_out, length = record
        first_out, first_back = jax.vjp(lambda v, p: encoder_layer(v, p, length), inputs.astype(jnp.float32), first_params)
        sent = low(first_out)
        second_out, second_back = jax.vjp(lambda v, p: encoder_layer(v, p, length), sent, second_params)
        second_dx, second_dp = second_back(grad_out.astype(jnp.float32))
        first_dx, first_dp = first_back(low(second_dx))
        totals = jax.tree.map(jnp.add, totals, (first_dp, second_dp))
        return (totals, (first_out.astype(jnp.bfloat16), second_out.astype(jnp.bfloat16), first_dx, second_dx))
    totals, stacked = lax.scan(one_clip, zeros, (flat_tokens, flat_cot, flat_lengths))
    first_out, second_out, first_dx, second_dx = stacked
    shape = (MB, CLIPS, LEN, D)
    layer_outputs = jnp.stack([first_out.reshape(shape), second_out.reshape(shape)])
    input_grads = jnp.stack([first_dx.reshape(shape), second_dx.reshape(shape)])
    merged = tuple((jnp.stack([totals[0][index], totals[1][index]]) for index in range(7)))
    return (layer_outputs, input_grads, merged[0], merged[1], merged[2], merged[3], merged[4], merged[5], merged[6])
```

```python
import functools
import math

import jax
import jax.numpy as jnp
from jax import lax
from jax.experimental import pallas as pl
from jax.experimental.pallas import tpu as pltpu
from jax.sharding import PartitionSpec as P

HD = 64
EPSILON = 1e-05
MASKED = -1e30
MESH = pl.DeviceIdType.MESH
F32 = jnp.float32
BF16 = jnp.bfloat16


def factor(count):
    side = 1
    while (2 * side) ** 3 <= count:
        side *= 2
    if count % (side * side):
        return (count, 1, 1)
    return (count // (side * side), side, side)


class Grid:
    def __init__(self, sizes):
        self.sizes = sizes
        slow, middle, fast = sizes
        me = lax.axis_index("dp")
        self.me = me
        self.z = me // (middle * fast)
        self.y = (me // fast) % middle
        self.x = me % fast

    def flat(self, z, y, x):
        return (z * self.sizes[1] + y) * self.sizes[2] + x

    def pair(self, z, y_first, a, b):
        return self.flat(z, a, b) if y_first else self.flat(z, b, a)

    def greet(self):
        slow, middle, fast = self.sizes
        barrier = pltpu.get_barrier_semaphore()
        peers = [self.flat((self.z + o) % slow, self.y, self.x) for o in range(1, slow)]
        peers += [self.flat(self.z, (self.y + o) % middle, self.x) for o in range(1, middle)]
        peers += [self.flat(self.z, self.y, (self.x + o) % fast) for o in range(1, fast)]
        for peer in peers:
            pl.semaphore_signal(barrier, inc=1, device_id={"dp": peer}, device_id_type=MESH)
        pl.semaphore_wait(barrier, len(peers))


def gather_kernel(sizes, count, *refs):
    shards, wholes = refs[:count], refs[count : 2 * count]
    send_sem, recv_sem, local_sem = refs[2 * count :]
    grid = Grid(sizes)
    slow = sizes[0]
    local = [
        pltpu.make_async_copy(shards[w], wholes[w].at[grid.me], local_sem.at[w])
        for w in range(count)
    ]
    for copy in local:
        copy.start()
    grid.greet()
    used = [0] * count
    sent = []

    def send(w, block, target):
        copy = pltpu.make_async_remote_copy(
            src_ref=wholes[w].at[block],
            dst_ref=wholes[w].at[block],
            send_sem=send_sem.at[w, used[w]],
            recv_sem=recv_sem.at[w, block],
            device_id={"dp": target},
            device_id_type=MESH,
        )
        copy.start()
        used[w] += 1
        sent.append(copy)

    def arrive(w, block):
        pltpu.make_async_remote_copy(
            src_ref=wholes[w].at[block],
            dst_ref=wholes[w].at[block],
            send_sem=send_sem.at[w, 0],
            recv_sem=recv_sem.at[w, block],
            device_id={"dp": grid.flat((grid.z + 1) % slow, grid.y, grid.x)},
            device_id_type=MESH,
        ).wait_recv()

    def place(z):
        y_first = z % 2 == 1
        if y_first:
            return True, grid.y, grid.x, sizes[1], sizes[2]
        return False, grid.x, grid.y, sizes[2], sizes[1]

    def first_stage(w):
        for z in range(slow):
            y_first, a, b, n_a, n_b = place(z)
            block = grid.flat(z, grid.y, grid.x)

            @pl.when(grid.z != z)
            def _():
                arrive(w, block)

            for o in range(1, n_a):
                send(w, block, grid.pair(grid.z, y_first, (a + o) % n_a, b))
            for o in range(1, n_b):
                send(w, block, grid.pair(grid.z, y_first, a, (b + o) % n_b))

    def second_stage(w):
        for z in range(slow):
            y_first, a, b, n_a, n_b = place(z)
            for o in range(1, n_a):
                block = grid.pair(z, y_first, (a + o) % n_a, b)
                arrive(w, block)
                for p in range(1, n_b):
                    send(w, block, grid.pair(grid.z, y_first, a, (b + p) % n_b))

    def third_stage(w):
        for z in range(slow):
            y_first, a, b, n_a, n_b = place(z)
            for o in range(n_a):
                for p in range(1, n_b):
                    arrive(w, grid.pair(z, y_first, (a + o) % n_a, (b + p) % n_b))

    for w in range(count):
        local[w].wait()
        for o in range(1, slow):
            send(w, grid.me, grid.flat((grid.z + o) % slow, grid.y, grid.x))
    for step in range(count + 1):
        if step < count:
            first_stage(step)
        if step >= 1:
            second_stage(step - 1)
    for w in range(count):
        third_stage(w)
    for copy in sent:
        copy.wait_send()


def gather_blocks(shards, sizes):
    total = sizes[0] * sizes[1] * sizes[2]
    count = len(shards)
    anywhere = pl.BlockSpec(memory_space=pl.ANY)
    return pl.pallas_call(
        functools.partial(gather_kernel, sizes, count),
        out_shape=[jax.ShapeDtypeStruct((total,) + s.shape, s.dtype) for s in shards],
        in_specs=[anywhere] * count,
        out_specs=[anywhere] * count,
        scratch_shapes=[
            pltpu.SemaphoreType.DMA((count, total)),
            pltpu.SemaphoreType.DMA((count, total)),
            pltpu.SemaphoreType.DMA((count,)),
        ],
        compiler_params=pltpu.CompilerParams(collective_id=0, has_side_effects=True),
        name="gather_blocks",
    )(*shards)


def scatter_kernel(sizes, count, *refs):
    terms, totals = refs[:count], refs[count : 2 * count]
    one, two, three = (refs[(2 + i) * count : (3 + i) * count] for i in range(3))
    send_sem, sem_one, sem_two, sem_three = refs[5 * count :]
    grid = Grid(sizes)
    slow = sizes[0]
    grid.greet()
    used = [0] * count
    sent = []

    def send(w, source, landing, semaphore, target):
        copy = pltpu.make_async_remote_copy(
            src_ref=source,
            dst_ref=landing,
            send_sem=send_sem.at[w, used[w]],
            recv_sem=semaphore,
            device_id={"dp": target},
            device_id_type=MESH,
        )
        copy.start()
        used[w] += 1
        sent.append(copy)

    def arrive(w, landing, semaphore):
        pltpu.make_async_remote_copy(
            src_ref=landing,
            dst_ref=landing,
            send_sem=send_sem.at[w, 0],
            recv_sem=semaphore,
            device_id={"dp": grid.flat((grid.z + 1) % slow, grid.y, grid.x)},
            device_id_type=MESH,
        ).wait_recv()

    def place(z):
        y_first = z % 2 == 0
        if y_first:
            return True, grid.y, grid.x, sizes[1], sizes[2]
        return False, grid.x, grid.y, sizes[2], sizes[1]

    def send_one(w):
        for z in range(slow):
            y_first, a, b, n_a, n_b = place(z)
            for o in range(1, n_a):
                far = (a + o) % n_a
                for p in range(n_b):
                    send(
                        w,
                        terms[w].at[grid.pair(z, y_first, far, p)],
                        one[w].at[z, o - 1, p],
                        sem_one.at[w, z, o - 1, p],
                        grid.pair(grid.z, y_first, far, b),
                    )

    def finish_one(w):
        for z in range(slow):
            y_first, a, b, n_a, n_b = place(z)
            for q in range(n_b):
                p = (b + 1 + q) % n_b
                for o in range(1, n_a):
                    arrive(w, one[w].at[z, o - 1, p], sem_one.at[w, z, o - 1, p])
                value = terms[w][grid.pair(z, y_first, a, p)].astype(F32)
                for o in range(1, n_a):
                    value = value + one[w][z, o - 1, p].astype(F32)
                one[w][z, 0, p] = value.astype(one[w].dtype)
                if q < n_b - 1:
                    send(
                        w,
                        one[w].at[z, 0, p],
                        two[w].at[z, q],
                        sem_two.at[w, z, q],
                        grid.pair(grid.z, y_first, a, p),
                    )

    def finish_two(w):
        for z in range(slow):
            y_first, a, b, n_a, n_b = place(z)
            for q in range(n_b - 1):
                arrive(w, two[w].at[z, q], sem_two.at[w, z, q])
            value = one[w][z, 0, b].astype(F32)
            for q in range(n_b - 1):
                value = value + two[w][z, q].astype(F32)
            two[w][z, 0] = value.astype(two[w].dtype)
        for o in range(1, slow):
            far = (grid.z + o) % slow
            send(
                w,
                two[w].at[far, 0],
                three[w].at[o - 1],
                sem_three.at[w, o - 1],
                grid.flat(far, grid.y, grid.x),
            )

    def finish_three(w):
        value = two[w][grid.z, 0].astype(F32)
        for o in range(1, slow):
            arrive(w, three[w].at[o - 1], sem_three.at[w, o - 1])
            value = value + three[w][o - 1].astype(F32)
        totals[w][...] = value

    for w in range(min(2, count)):
        send_one(w)
    for step in range(count + 2):
        if step < count:
            finish_one(step)
        if step + 2 < count:
            send_one(step + 2)
        if 1 <= step <= count:
            finish_two(step - 1)
        if step >= 2:
            finish_three(step - 2)
    for copy in sent:
        copy.wait_send()


def scatter_blocks(terms, sizes):
    slow, middle, fast = sizes
    total = slow * middle * fast
    count = len(terms)
    inside = pl.BlockSpec(memory_space=pltpu.VMEM)
    return pl.pallas_call(
        functools.partial(scatter_kernel, sizes, count),
        out_shape=[jax.ShapeDtypeStruct(t.shape[1:], F32) for t in terms],
        in_specs=[inside] * count,
        out_specs=[inside] * count,
        scratch_shapes=[
            pltpu.VMEM((slow, middle - 1, middle) + t.shape[1:], t.dtype) for t in terms
        ]
        + [pltpu.VMEM((slow, middle - 1) + t.shape[1:], t.dtype) for t in terms]
        + [pltpu.VMEM((slow - 1,) + t.shape[1:], t.dtype) for t in terms]
        + [
            pltpu.SemaphoreType.DMA((count, total)),
            pltpu.SemaphoreType.DMA((count, slow, middle - 1, middle)),
            pltpu.SemaphoreType.DMA((count, slow, middle - 1)),
            pltpu.SemaphoreType.DMA((count, slow - 1)),
        ],
        compiler_params=pltpu.CompilerParams(
            collective_id=1, has_side_effects=True, vmem_limit_bytes=48 * 1024 * 1024
        ),
        name="scatter_blocks",
    )(*terms)


def contract_rows(left, right):
    return lax.dot_general(left, right, (((0,), (0,)), ((), ())), preferred_element_type=F32)


def contract_cols(left, right):
    return lax.dot_general(left, right, (((1,), (1,)), ((), ())), preferred_element_type=F32)


def standardize(values):
    centred = values - jnp.mean(values, -1, keepdims=True)
    variance = jnp.mean(centred * centred, -1, keepdims=True)
    inverse = lax.rsqrt(variance + EPSILON)
    return centred * inverse, inverse


def norm_backward(grad_out, standard, inverse, gain):
    scaled = grad_out * gain
    return inverse * (
        scaled
        - jnp.mean(scaled, -1, keepdims=True)
        - standard * jnp.mean(scaled * standard, -1, keepdims=True)
    )


def normal_cdf(values):
    return 0.5 * (1.0 + lax.erf(values * math.sqrt(0.5)))


def by_head(values, clips):
    rows, width = values.shape
    return values.reshape(clips, rows // clips, width // HD, HD).transpose(0, 2, 1, 3)


def by_row(values):
    clips, heads, frames, size = values.shape
    return values.transpose(0, 2, 1, 3).reshape(clips * frames, heads * size)


def scores_of(query, keyed, visible):
    scores = jnp.einsum("chqd,chkd->chqk", query, keyed, preferred_element_type=F32)
    return jnp.where(visible, scores * (1.0 / math.sqrt(HD)), MASKED)


def layer_forward(source, visible, clips, weights):
    qkv_weight, out_weight, up_weight, down_weight, up_bias, gains, biases = weights
    width = source.shape[1]
    inputs = source.astype(F32)
    standard, inverse = standardize(inputs)
    normed = (standard * gains[0] + biases[0]).astype(BF16)
    mixed = jnp.dot(normed, qkv_weight, preferred_element_type=F32)
    query = by_head((mixed[:, :width] + biases[1]).astype(BF16), clips)
    keyed = by_head(mixed[:, width : 2 * width].astype(BF16), clips)
    valued = by_head((mixed[:, 2 * width :] + biases[2]).astype(BF16), clips)
    scores = scores_of(query, keyed, visible)
    largest = jnp.max(scores, -1, keepdims=True)
    exponent = jnp.exp(scores - largest)
    total = jnp.sum(exponent, -1, keepdims=True)
    probability = (exponent / total).astype(BF16)
    context = jnp.einsum("chqk,chkd->chqd", probability, valued, preferred_element_type=F32)
    context = by_row(context.astype(BF16))
    log_total = largest + jnp.log(total)
    hidden = inputs + (jnp.dot(context, out_weight, preferred_element_type=F32) + biases[3])
    standard_two, inverse_two = standardize(hidden)
    normed_two = (standard_two * gains[1] + biases[4]).astype(BF16)
    upper = jnp.dot(normed_two, up_weight, preferred_element_type=F32) + up_bias
    active = (upper * normal_cdf(upper)).astype(BF16)
    result = hidden + (jnp.dot(active, down_weight, preferred_element_type=F32) + biases[5])
    saved = (
        (standard, inverse, normed, query, keyed, valued, log_total, context)
        + (standard_two, inverse_two, normed_two, upper, active)
    )
    return result.astype(BF16), saved


def layer_backward(grad_half, saved, visible, clips, weights):
    qkv_weight, out_weight, up_weight, down_weight, up_bias, gains, biases = weights
    standard, inverse, normed, query, keyed, valued, log_total, context = saved[:8]
    standard_two, inverse_two, normed_two, upper, active = saved[8:]
    scaling = 1.0 / math.sqrt(HD)
    grad_out = grad_half.astype(F32)
    active_grad = contract_cols(grad_half, down_weight)
    density = jnp.exp(-0.5 * upper * upper) * (1.0 / math.sqrt(2.0 * math.pi))
    upper_grad = (active_grad * (normal_cdf(upper) + upper * density)).astype(BF16)
    normed_two_grad = contract_cols(upper_grad, up_weight)
    hidden_grad = grad_out + norm_backward(normed_two_grad, standard_two, inverse_two, gains[1])
    branch_grad = hidden_grad.astype(BF16)
    context_grad = by_head(contract_cols(branch_grad, out_weight).astype(BF16), clips)
    probability = jnp.exp(scores_of(query, keyed, visible) - log_total)
    value_grad = jnp.einsum(
        "chqk,chqd->chkd", probability.astype(BF16), context_grad, preferred_element_type=F32
    )
    prob_grad = jnp.einsum("chqd,chkd->chqk", context_grad, valued, preferred_element_type=F32)
    inner = jnp.sum(probability * prob_grad, -1, keepdims=True)
    score_grad = (probability * (prob_grad - inner)).astype(BF16)
    query_grad = scaling * jnp.einsum(
        "chqk,chkd->chqd", score_grad, keyed, preferred_element_type=F32
    )
    key_grad = scaling * jnp.einsum(
        "chqk,chqd->chkd", score_grad, query, preferred_element_type=F32
    )
    mixed_grad = jnp.concatenate(
        [by_row(part.astype(BF16)) for part in (query_grad, key_grad, value_grad)], 1
    )
    normed_grad = contract_cols(mixed_grad, qkv_weight)
    input_grad = hidden_grad + norm_backward(normed_grad, standard, inverse, gains[0])
    return input_grad, (upper_grad, normed_two_grad, branch_grad, mixed_grad, normed_grad)


def weight_terms(grad_half, saved, grads):
    standard, normed, context = saved[0], saved[2], saved[7]
    standard_two, normed_two, active = saved[8], saved[10], saved[12]
    upper_grad, normed_two_grad, branch_grad, mixed_grad, normed_grad = grads
    width = standard.shape[1]
    large = (
        contract_rows(normed, mixed_grad),
        contract_rows(context, branch_grad),
        contract_rows(normed_two, upper_grad),
        contract_rows(active, grad_half),
    )
    mixed_sum = jnp.sum(mixed_grad.astype(F32), 0)
    gains = jnp.stack(
        [jnp.sum(normed_grad * standard, 0), jnp.sum(normed_two_grad * standard_two, 0)]
    )
    biases = jnp.stack(
        [
            jnp.sum(normed_grad, 0),
            mixed_sum[:width],
            mixed_sum[2 * width :],
            jnp.sum(branch_grad.astype(F32), 0),
            jnp.sum(normed_two_grad, 0),
            jnp.sum(grad_half.astype(F32), 0),
        ]
    )
    return large, (jnp.sum(upper_grad.astype(F32), 0), gains, biases)


def gather_weights(large, small, sizes):
    total = sizes[0] * sizes[1] * sizes[2]
    if any(entry.shape[0] % 16 for entry in large) or min(sizes) < 2:
        return tuple(lax.all_gather(entry, "dp", axis=0, tiled=True) for entry in large) + tuple(
            lax.all_gather(entry, "dp", axis=entry.ndim - 1, tiled=True) for entry in small
        )
    flat = jnp.concatenate([entry.reshape(-1) for entry in small])
    room = -(-flat.size // 2048) * 2048
    packed = jnp.pad(flat, (0, room - flat.size)).reshape(-1, 128)
    *wholes, joined = gather_blocks(tuple(large[i] for i in (0, 1, 2, 3)) + (packed,), sizes)
    joined = joined.reshape(total, room)
    result = [whole.reshape(-1, whole.shape[2]) for whole in wholes]
    start = 0
    for entry in small:
        piece = joined[:, start : start + entry.size].reshape((total,) + entry.shape)
        result.append(jnp.moveaxis(piece, 0, -2).reshape(entry.shape[:-1] + (-1,)))
        start += entry.size
    return tuple(result)


def scatter_terms(large, small, sizes):
    total = sizes[0] * sizes[1] * sizes[2]
    if any((entry.shape[0] // total) % 16 for entry in large) or min(sizes) < 2:
        return tuple(
            lax.psum_scatter(entry, "dp", scatter_dimension=0, tiled=True) for entry in large
        ) + tuple(
            lax.psum_scatter(entry, "dp", scatter_dimension=entry.ndim - 1, tiled=True)
            for entry in small
        )
    blocks = [entry.astype(BF16).reshape(total, -1, entry.shape[1]) for entry in large]
    pieces = [
        jnp.moveaxis(entry.reshape(entry.shape[:-1] + (total, -1)), -2, 0).reshape(total, -1)
        for entry in small
    ]
    flat = jnp.concatenate(pieces, 1)
    room = -(-flat.shape[1] // 1024) * 1024
    packed = jnp.pad(flat, ((0, 0), (0, room - flat.shape[1]))).reshape(total, -1, 128)
    *owned, joined = scatter_blocks(blocks + [packed], sizes)
    joined = joined.reshape(-1)
    start = 0
    for entry in small:
        size = entry.size // total
        owned.append(joined[start : start + size].reshape(entry.shape[:-1] + (-1,)))
        start += size
    return tuple(owned)


def on_device(
    sizes,
    tokens,
    cotangent,
    lengths,
    qkv_weight,
    out_weight,
    up_weight,
    down_weight,
    up_bias,
    norm_gains,
    biases,
):
    is_first = lax.axis_index("section") == 0
    micro_count, own_clips, frames, width = tokens.shape
    clips = micro_count * own_clips
    own_tokens = tokens.reshape(clips * frames, width)
    own_cot = cotangent.reshape(clips * frames, width)
    visible = (jnp.arange(frames)[None, :] < lengths.reshape(clips, 1))[:, None, None, :]
    weights = gather_weights(
        (qkv_weight[0], out_weight[0], up_weight[0], down_weight[0]),
        (up_bias[0], norm_gains[0], biases[0]),
        sizes,
    )
    weights = weights[:4] + tuple(entry.astype(F32) for entry in weights[4:])

    early = layer_forward(own_tokens, visible, clips, weights)[0]
    handed = lax.ppermute(early, "section", [(0, 1)])
    source = jnp.where(is_first, own_tokens, handed)
    output, saved = layer_forward(source, visible, clips, weights)
    late = layer_backward(own_cot, saved, visible, clips, weights)[0]
    returned = lax.ppermute(late.astype(BF16), "section", [(1, 0)])
    grad_half = jnp.where(is_first, returned, own_cot)
    input_grad, grads = layer_backward(grad_half, saved, visible, clips, weights)
    owned = scatter_terms(*weight_terms(grad_half, saved, grads), sizes)
    out_shape = (1, micro_count, own_clips, frames, width)
    return (output.reshape(out_shape), input_grad.reshape(out_shape)) + tuple(
        entry[None] for entry in owned
    )


def solution(mesh):
    sizes = factor(mesh.shape["dp"])
    placed = (
        P(None, "dp", None, None),
        P(None, "dp", None, None),
        P(None, "dp"),
        P("section", "dp", None),
        P("section", "dp", None),
        P("section", "dp", None),
        P("section", "dp", None),
        P("section", "dp"),
        P("section", None, "dp"),
        P("section", None, "dp"),
    )
    return jax.shard_map(
        functools.partial(on_device, sizes),
        mesh=mesh,
        in_specs=placed,
        out_specs=(
            P("section", None, "dp", None, None),
            P("section", None, "dp", None, None),
            P("section", "dp", None),
            P("section", "dp", None),
            P("section", "dp", None),
            P("section", "dp", None),
            P("section", "dp"),
            P("section", None, "dp"),
            P("section", None, "dp"),
        ),
        check_vma=False,
    )
```

```python
import functools
import math

import jax
import jax.numpy as jnp
from jax import lax
from jax.experimental import pallas as pl
from jax.experimental.pallas import tpu as pltpu
from jax.sharding import PartitionSpec as P

HD = 64
EPSILON = 1e-05
MASKED = -1e30
PARTS = 3
AHEAD = 2
MESH = pl.DeviceIdType.MESH
F32 = jnp.float32
BF16 = jnp.bfloat16


def factor(count):
    side = 1
    while (2 * side) ** 3 <= count:
        side *= 2
    if count % (side * side):
        return (count, 1, 1)
    return (count // (side * side), side, side)


def cut(rows, parts):
    while rows % (16 * parts):
        parts -= 1
    return [(i * (rows // parts), rows // parts) for i in range(parts)]


def all_pieces(shapes):
    room = [shape[-1] * shape[-2] for shape in shapes]
    pieces = []
    for w in sorted(range(len(shapes)), key=lambda w: -room[w]):
        parts = PARTS if 2 * room[w] > max(room) else 1
        if parts > 1:
            pieces += [(w,) + rows for rows in cut(shapes[w][-2], parts)]
        else:
            pieces.append((w, 0, shapes[w][-2]))
    return pieces


def nearest_first(length):
    return sorted(range(length), key=lambda offset: min(offset, length - offset))


class Grid:
    def __init__(self, sizes):
        self.sizes = sizes
        slow, middle, fast = sizes
        me = lax.axis_index("dp")
        self.me = me
        self.z = me // (middle * fast)
        self.y = (me // fast) % middle
        self.x = me % fast

    def flat(self, z, y, x):
        return (z * self.sizes[1] + y) * self.sizes[2] + x

    def plane(self, offset, odd):
        side = self.sizes[1]
        z = (self.z + offset) % self.sizes[0]
        turned = (z + odd) % 2
        a = turned * self.y + (1 - turned) * self.x
        b = turned * self.x + (1 - turned) * self.y
        return z, a, b, turned * side + (1 - turned), turned + (1 - turned) * side

    def greet(self):
        slow, middle, fast = self.sizes
        barrier = pltpu.get_barrier_semaphore()
        peers = [self.flat((self.z + o) % slow, self.y, self.x) for o in range(1, slow)]
        peers += [self.flat(self.z, (self.y + o) % middle, self.x) for o in range(1, middle)]
        peers += [self.flat(self.z, self.y, (self.x + o) % fast) for o in range(1, fast)]
        for peer in peers:
            pl.semaphore_signal(barrier, inc=1, device_id={"dp": peer}, device_id_type=MESH)
        pl.semaphore_wait(barrier, len(peers))


def gather_kernel(sizes, count, *refs):
    shards, wholes = refs[:count], refs[count : 2 * count]
    send_sem, recv_sem, local_sem = refs[2 * count :]
    grid = Grid(sizes)
    slow, side = sizes[0], sizes[1]
    turns = nearest_first(slow)
    local = [
        pltpu.make_async_copy(shards[w], wholes[w].at[grid.me], local_sem.at[w])
        for w in range(count)
    ]
    for copy in local:
        copy.start()
    pieces = all_pieces([shard.shape for shard in shards])
    grid.greet()
    used = [0] * len(pieces)
    sent = []

    def part(i, block):
        w, start, size = pieces[i]
        return wholes[w].at[block, pl.ds(start, size), :]

    def send(w, block, target):
        copy = pltpu.make_async_remote_copy(
            src_ref=part(w, block),
            dst_ref=part(w, block),
            send_sem=send_sem.at[w, used[w]],
            recv_sem=recv_sem.at[w, block],
            device_id={"dp": target},
            device_id_type=MESH,
        )
        copy.start()
        used[w] += 1
        sent.append(copy)

    def arrive(w, block):
        pltpu.make_async_remote_copy(
            src_ref=part(w, block),
            dst_ref=part(w, block),
            send_sem=send_sem.at[w, 0],
            recv_sem=recv_sem.at[w, block],
            device_id={"dp": grid.flat((grid.z + 1) % slow, grid.y, grid.x)},
            device_id_type=MESH,
        ).wait_recv()

    def spread(w, block):
        for o in range(1, sizes[2]):
            send(w, block, grid.flat(grid.z, grid.y, (grid.x + o) % sizes[2]))
        for o in range(1, sizes[1]):
            send(w, block, grid.flat(grid.z, (grid.y + o) % sizes[1], grid.x))

    def second_stage(w):
        for offset in turns:
            z, a, b, unit_a, unit_b = grid.plane(offset, 0)
            for o in range(1, side):
                block = z * side * side + (a + o) % side * unit_a + b * unit_b
                arrive(w, block)
                for p in range(1, side):
                    target = grid.z * side * side + a * unit_a + (b + p) % side * unit_b
                    send(w, block, target)

    def third_stage(w):
        for offset in turns:
            z, a, b, unit_a, unit_b = grid.plane(offset, 0)
            for o in range(side):
                for p in range(1, side):
                    arrive(
                        w, z * side * side + (a + o) % side * unit_a + (b + p) % side * unit_b
                    )

    def first_stage(w):
        for offset in turns[1:]:
            block = grid.flat((grid.z + offset) % slow, grid.y, grid.x)
            arrive(w, block)
            spread(w, block)

    for copy in local:
        copy.wait()
    for w in range(len(pieces)):
        for offset in turns[1:]:
            send(w, grid.me, grid.flat((grid.z + offset) % slow, grid.y, grid.x))
        spread(w, grid.me)
    for step in range(len(pieces) + 1):
        if step < len(pieces):
            first_stage(step)
        if step >= 1:
            second_stage(step - 1)
    for w in range(len(pieces)):
        third_stage(w)
    for copy in sent:
        copy.wait_send()


def gather_blocks(shards, sizes):
    total = sizes[0] * sizes[1] * sizes[2]
    count = len(shards)
    pieces = len(all_pieces([shard.shape for shard in shards]))
    anywhere = pl.BlockSpec(memory_space=pl.ANY)
    return pl.pallas_call(
        functools.partial(gather_kernel, sizes, count),
        out_shape=[jax.ShapeDtypeStruct((total,) + s.shape, s.dtype) for s in shards],
        in_specs=[anywhere] * count,
        out_specs=[anywhere] * count,
        scratch_shapes=[
            pltpu.SemaphoreType.DMA((pieces, total)),
            pltpu.SemaphoreType.DMA((pieces, total)),
            pltpu.SemaphoreType.DMA((count,)),
        ],
        compiler_params=pltpu.CompilerParams(collective_id=0, has_side_effects=True),
        name="gather_blocks",
    )(*shards)


def scatter_kernel(sizes, count, *refs):
    terms, totals = refs[:count], refs[count : 2 * count]
    held = tuple(refs[(2 + i) * count : (3 + i) * count] for i in range(3))
    send_sem, sem_one, sem_two, sem_three = refs[5 * count :]
    grid = Grid(sizes)
    slow, side = sizes[0], sizes[1]
    turns = nearest_first(slow)[::-1]
    grid.greet()
    pieces = all_pieces([term.shape for term in terms])
    used = [0] * len(pieces)
    sent = []

    def rows(arrays):
        return [arrays[w].at[..., pl.ds(start, size), :] for w, start, size in pieces]

    terms, totals, one, two, three = (
        rows(arrays) for arrays in (terms, totals) + held
    )

    def send(w, source, landing, semaphore, target):
        copy = pltpu.make_async_remote_copy(
            src_ref=source,
            dst_ref=landing,
            send_sem=send_sem.at[w, used[w]],
            recv_sem=semaphore,
            device_id={"dp": target},
            device_id_type=MESH,
        )
        copy.start()
        used[w] += 1
        sent.append(copy)

    def arrive(w, landing, semaphore):
        pltpu.make_async_remote_copy(
            src_ref=landing,
            dst_ref=landing,
            send_sem=send_sem.at[w, 0],
            recv_sem=semaphore,
            device_id={"dp": grid.flat((grid.z + 1) % slow, grid.y, grid.x)},
            device_id_type=MESH,
        ).wait_recv()

    def send_one(w):
        for offset in turns:
            z, a, b, unit_a, unit_b = grid.plane(offset, 1)
            for o in range(1, side):
                far = (a + o) % side
                for q in range(side):
                    p = (b + 1 + q) % side
                    send(
                        w,
                        terms[w].at[z * side * side + far * unit_a + p * unit_b],
                        one[w].at[offset, o - 1, p],
                        sem_one.at[w, offset, o - 1, p],
                        grid.z * side * side + far * unit_a + b * unit_b,
                    )

    def finish_one(w):
        for offset in turns:
            z, a, b, unit_a, unit_b = grid.plane(offset, 1)
            for q in range(side):
                p = (b + 1 + q) % side
                for o in range(1, side):
                    arrive(w, one[w].at[offset, o - 1, p], sem_one.at[w, offset, o - 1, p])
                value = terms[w][z * side * side + a * unit_a + p * unit_b].astype(F32)
                for o in range(1, side):
                    value = value + one[w][offset, o - 1, p].astype(F32)
                one[w][offset, 0, p] = value.astype(one[w].dtype)
                if q < side - 1:
                    send(
                        w,
                        one[w].at[offset, 0, p],
                        two[w].at[offset, q],
                        sem_two.at[w, offset, q],
                        grid.z * side * side + a * unit_a + p * unit_b,
                    )

    def finish_two(w):
        for offset in turns:
            z, a, b, unit_a, unit_b = grid.plane(offset, 1)
            for q in range(side - 1):
                arrive(w, two[w].at[offset, q], sem_two.at[w, offset, q])
            value = one[w][offset, 0, b].astype(F32)
            for q in range(side - 1):
                value = value + two[w][offset, q].astype(F32)
            two[w][offset, 0] = value.astype(two[w].dtype)
            if offset:
                send(
                    w,
                    two[w].at[offset, 0],
                    three[w].at[offset - 1],
                    sem_three.at[w, offset - 1],
                    grid.flat(z, grid.y, grid.x),
                )

    def finish_three(w):
        value = two[w][0, 0].astype(F32)
        for o in range(1, slow):
            arrive(w, three[w].at[o - 1], sem_three.at[w, o - 1])
            value = value + three[w][o - 1].astype(F32)
        totals[w][...] = value

    ahead = min(AHEAD, len(pieces))
    for w in range(ahead):
        send_one(w)
    for step in range(len(pieces) + 2):
        if step < len(pieces):
            finish_one(step)
        if step + ahead < len(pieces):
            send_one(step + ahead)
        if 1 <= step <= len(pieces):
            finish_two(step - 1)
        if step >= 2:
            finish_three(step - 2)
    for copy in sent:
        copy.wait_send()


def scatter_blocks(terms, sizes):
    slow, middle, fast = sizes
    total = slow * middle * fast
    count = len(terms)
    pieces = len(all_pieces([term.shape for term in terms]))
    inside = pl.BlockSpec(memory_space=pltpu.VMEM)
    return pl.pallas_call(
        functools.partial(scatter_kernel, sizes, count),
        out_shape=[jax.ShapeDtypeStruct(t.shape[1:], F32) for t in terms],
        in_specs=[inside] * count,
        out_specs=[inside] * count,
        scratch_shapes=[
            pltpu.VMEM((slow, middle - 1, middle) + t.shape[1:], t.dtype) for t in terms
        ]
        + [pltpu.VMEM((slow, middle - 1) + t.shape[1:], t.dtype) for t in terms]
        + [pltpu.VMEM((slow - 1,) + t.shape[1:], t.dtype) for t in terms]
        + [
            pltpu.SemaphoreType.DMA((pieces, total)),
            pltpu.SemaphoreType.DMA((pieces, slow, middle - 1, middle)),
            pltpu.SemaphoreType.DMA((pieces, slow, middle - 1)),
            pltpu.SemaphoreType.DMA((pieces, slow - 1)),
        ],
        compiler_params=pltpu.CompilerParams(
            collective_id=1, has_side_effects=True, vmem_limit_bytes=48 * 1024 * 1024
        ),
        name="scatter_blocks",
    )(*terms)


def contract_rows(left, right):
    return lax.dot_general(left, right, (((0,), (0,)), ((), ())), preferred_element_type=F32)


def contract_cols(left, right):
    return lax.dot_general(left, right, (((1,), (1,)), ((), ())), preferred_element_type=F32)


def standardize(values):
    centred = values - jnp.mean(values, -1, keepdims=True)
    variance = jnp.mean(centred * centred, -1, keepdims=True)
    inverse = lax.rsqrt(variance + EPSILON)
    return centred * inverse, inverse


def norm_backward(grad_out, standard, inverse, gain):
    scaled = grad_out * gain
    return inverse * (
        scaled
        - jnp.mean(scaled, -1, keepdims=True)
        - standard * jnp.mean(scaled * standard, -1, keepdims=True)
    )


def normal_cdf(values):
    return 0.5 * (1.0 + lax.erf(values * math.sqrt(0.5)))


def by_head(values, clips):
    rows, width = values.shape
    return values.reshape(clips, rows // clips, width // HD, HD).transpose(0, 2, 1, 3)


def by_row(values):
    clips, heads, frames, size = values.shape
    return values.transpose(0, 2, 1, 3).reshape(clips * frames, heads * size)


def scores_of(query, keyed, visible):
    scores = jnp.einsum("chqd,chkd->chqk", query, keyed, preferred_element_type=F32)
    return jnp.where(visible, scores * (1.0 / math.sqrt(HD)), MASKED)


def layer_forward(source, visible, clips, weights):
    qkv_weight, out_weight, up_weight, down_weight, up_bias, gains, biases = weights
    width = source.shape[1]
    inputs = source.astype(F32)
    standard, inverse = standardize(inputs)
    normed = (standard * gains[0] + biases[0]).astype(BF16)
    mixed = jnp.dot(normed, qkv_weight, preferred_element_type=F32)
    query = by_head((mixed[:, :width] + biases[1]).astype(BF16), clips)
    keyed = by_head(mixed[:, width : 2 * width].astype(BF16), clips)
    valued = by_head((mixed[:, 2 * width :] + biases[2]).astype(BF16), clips)
    scores = scores_of(query, keyed, visible)
    largest = jnp.max(scores, -1, keepdims=True)
    exponent = jnp.exp(scores - largest)
    total = jnp.sum(exponent, -1, keepdims=True)
    probability = (exponent / total).astype(BF16)
    context = jnp.einsum("chqk,chkd->chqd", probability, valued, preferred_element_type=F32)
    context = by_row(context.astype(BF16))
    log_total = largest + jnp.log(total)
    hidden = inputs + (jnp.dot(context, out_weight, preferred_element_type=F32) + biases[3])
    standard_two, inverse_two = standardize(hidden)
    normed_two = (standard_two * gains[1] + biases[4]).astype(BF16)
    upper = jnp.dot(normed_two, up_weight, preferred_element_type=F32) + up_bias
    active = (upper * normal_cdf(upper)).astype(BF16)
    result = hidden + (jnp.dot(active, down_weight, preferred_element_type=F32) + biases[5])
    saved = (
        (standard, inverse, normed, query, keyed, valued, log_total, context)
        + (standard_two, inverse_two, normed_two, upper, active)
    )
    return result.astype(BF16), saved


def layer_backward(grad_half, saved, visible, clips, weights):
    qkv_weight, out_weight, up_weight, down_weight, up_bias, gains, biases = weights
    standard, inverse, normed, query, keyed, valued, log_total, context = saved[:8]
    standard_two, inverse_two, normed_two, upper, active = saved[8:]
    scaling = 1.0 / math.sqrt(HD)
    grad_out = grad_half.astype(F32)
    active_grad = contract_cols(grad_half, down_weight)
    density = jnp.exp(-0.5 * upper * upper) * (1.0 / math.sqrt(2.0 * math.pi))
    upper_grad = (active_grad * (normal_cdf(upper) + upper * density)).astype(BF16)
    normed_two_grad = contract_cols(upper_grad, up_weight)
    hidden_grad = grad_out + norm_backward(normed_two_grad, standard_two, inverse_two, gains[1])
    branch_grad = hidden_grad.astype(BF16)
    context_grad = by_head(contract_cols(branch_grad, out_weight).astype(BF16), clips)
    probability = jnp.exp(scores_of(query, keyed, visible) - log_total)
    value_grad = jnp.einsum(
        "chqk,chqd->chkd", probability.astype(BF16), context_grad, preferred_element_type=F32
    )
    prob_grad = jnp.einsum("chqd,chkd->chqk", context_grad, valued, preferred_element_type=F32)
    inner = jnp.sum(probability * prob_grad, -1, keepdims=True)
    score_grad = (probability * (prob_grad - inner)).astype(BF16)
    query_grad = scaling * jnp.einsum(
        "chqk,chkd->chqd", score_grad, keyed, preferred_element_type=F32
    )
    key_grad = scaling * jnp.einsum(
        "chqk,chqd->chkd", score_grad, query, preferred_element_type=F32
    )
    mixed_grad = jnp.concatenate(
        [by_row(part.astype(BF16)) for part in (query_grad, key_grad, value_grad)], 1
    )
    normed_grad = contract_cols(mixed_grad, qkv_weight)
    input_grad = hidden_grad + norm_backward(normed_grad, standard, inverse, gains[0])
    return input_grad, (upper_grad, normed_two_grad, branch_grad, mixed_grad, normed_grad)


def weight_terms(grad_half, saved, grads):
    standard, normed, context = saved[0], saved[2], saved[7]
    standard_two, normed_two, active = saved[8], saved[10], saved[12]
    upper_grad, normed_two_grad, branch_grad, mixed_grad, normed_grad = grads
    width = standard.shape[1]
    large = (
        contract_rows(normed, mixed_grad),
        contract_rows(context, branch_grad),
        contract_rows(normed_two, upper_grad),
        contract_rows(active, grad_half),
    )
    mixed_sum = jnp.sum(mixed_grad.astype(F32), 0)
    gains = jnp.stack(
        [jnp.sum(normed_grad * standard, 0), jnp.sum(normed_two_grad * standard_two, 0)]
    )
    biases = jnp.stack(
        [
            jnp.sum(normed_grad, 0),
            mixed_sum[:width],
            mixed_sum[2 * width :],
            jnp.sum(branch_grad.astype(F32), 0),
            jnp.sum(normed_two_grad, 0),
            jnp.sum(grad_half.astype(F32), 0),
        ]
    )
    return large, (jnp.sum(upper_grad.astype(F32), 0), gains, biases)


def gather_weights(large, small, sizes):
    total = sizes[0] * sizes[1] * sizes[2]
    if any(entry.shape[0] % 16 for entry in large) or min(sizes) < 2:
        return tuple(lax.all_gather(entry, "dp", axis=0, tiled=True) for entry in large) + tuple(
            lax.all_gather(entry, "dp", axis=entry.ndim - 1, tiled=True) for entry in small
        )
    flat = jnp.concatenate([entry.reshape(-1) for entry in small])
    room = -(-flat.size // 2048) * 2048
    packed = jnp.pad(flat, (0, room - flat.size)).reshape(-1, 128)
    *wholes, joined = gather_blocks(tuple(large[i] for i in (0, 1, 2, 3)) + (packed,), sizes)
    joined = joined.reshape(total, room)
    result = [whole.reshape(-1, whole.shape[2]) for whole in wholes]
    start = 0
    for entry in small:
        piece = joined[:, start : start + entry.size].reshape((total,) + entry.shape)
        result.append(jnp.moveaxis(piece, 0, -2).reshape(entry.shape[:-1] + (-1,)))
        start += entry.size
    return tuple(result)


def scatter_terms(large, small, sizes):
    total = sizes[0] * sizes[1] * sizes[2]
    if any((entry.shape[0] // total) % 16 for entry in large) or min(sizes) < 2:
        return tuple(
            lax.psum_scatter(entry, "dp", scatter_dimension=0, tiled=True) for entry in large
        ) + tuple(
            lax.psum_scatter(entry, "dp", scatter_dimension=entry.ndim - 1, tiled=True)
            for entry in small
        )
    blocks = [entry.astype(BF16).reshape(total, -1, entry.shape[1]) for entry in large]
    pieces = [
        jnp.moveaxis(entry.reshape(entry.shape[:-1] + (total, -1)), -2, 0).reshape(total, -1)
        for entry in small
    ]
    flat = jnp.concatenate(pieces, 1)
    room = -(-flat.shape[1] // 1024) * 1024
    packed = jnp.pad(flat, ((0, 0), (0, room - flat.shape[1]))).reshape(total, -1, 128)
    *owned, joined = scatter_blocks(blocks + [packed], sizes)
    joined = joined.reshape(-1)
    start = 0
    for entry in small:
        size = entry.size // total
        owned.append(joined[start : start + size].reshape(entry.shape[:-1] + (-1,)))
        start += size
    return tuple(owned)


def on_device(
    sizes,
    tokens,
    cotangent,
    lengths,
    qkv_weight,
    out_weight,
    up_weight,
    down_weight,
    up_bias,
    norm_gains,
    biases,
):
    is_first = lax.axis_index("section") == 0
    micro_count, own_clips, frames, width = tokens.shape
    clips = micro_count * own_clips
    own_tokens = tokens.reshape(clips * frames, width)
    own_cot = cotangent.reshape(clips * frames, width)
    visible = (jnp.arange(frames)[None, :] < lengths.reshape(clips, 1))[:, None, None, :]
    weights = gather_weights(
        (qkv_weight[0], out_weight[0], up_weight[0], down_weight[0]),
        (up_bias[0], norm_gains[0], biases[0]),
        sizes,
    )
    weights = weights[:4] + tuple(entry.astype(F32) for entry in weights[4:])

    early = lax.cond(
        is_first,
        lambda: layer_forward(own_tokens, visible, clips, weights)[0],
        lambda: jnp.zeros_like(own_tokens),
    )
    handed = lax.ppermute(early, "section", [(0, 1)])
    source = jnp.where(is_first, own_tokens, handed)
    output, saved = layer_forward(source, visible, clips, weights)
    late = layer_backward(own_cot, saved, visible, clips, weights)
    returned = lax.ppermute(late[0].astype(BF16), "section", [(1, 0)])
    grad_half = jnp.where(is_first, returned, own_cot)
    input_grad, grads = lax.cond(
        is_first,
        lambda: layer_backward(grad_half, saved, visible, clips, weights),
        lambda: late,
    )
    owned = scatter_terms(*weight_terms(grad_half, saved, grads), sizes)
    out_shape = (1, micro_count, own_clips, frames, width)
    return (output.reshape(out_shape), input_grad.reshape(out_shape)) + tuple(
        entry[None] for entry in owned
    )


def solution(mesh):
    sizes = factor(mesh.shape["dp"])
    placed = (
        P(None, "dp", None, None),
        P(None, "dp", None, None),
        P(None, "dp"),
        P("section", "dp", None),
        P("section", "dp", None),
        P("section", "dp", None),
        P("section", "dp", None),
        P("section", "dp"),
        P("section", None, "dp"),
        P("section", None, "dp"),
    )
    return jax.shard_map(
        functools.partial(on_device, sizes),
        mesh=mesh,
        in_specs=placed,
        out_specs=(
            P("section", None, "dp", None, None),
            P("section", None, "dp", None, None),
            P("section", "dp", None),
            P("section", "dp", None),
            P("section", "dp", None),
            P("section", "dp", None),
            P("section", "dp"),
            P("section", None, "dp"),
            P("section", None, "dp"),
        ),
        check_vma=False,
    )
```
